32 devices in a mesh: rep: 2 (over x), yz: 8 (over z, y), gx: 2 (over core).
Axes of the slice: x: 2, y: 2, z: 4, core: 2. Of those that a mesh axis runs over, the one named last changes fastest.
Arguments:
- tokens: bfloat16 [64, 3, 18432], P(('rep', 'yz'), None, 'gx'), parts along dimension 0, may hold values from -6 to 6
- query_weight: bfloat16 [18432, 2048], P('gx', 'yz'), may hold values from -0.046875 to 0.046875
- key_weight: bfloat16 [18432, 256], P('gx', 'yz'), may hold values from -0.3125 to 0.3125
- value_weight: bfloat16 [18432, 256], P('gx', 'yz'), may hold values from -0.046875 to 0.046875
- out_weight: bfloat16 [2048, 18432], P('yz', 'gx'), may hold values from -0.125 to 0.125
- key_cache: bfloat16 [64, 1536, 256], P(('rep', 'yz', 'gx')), parts along dimension 0, may hold values from -600 to 600
- value_cache: bfloat16 [64, 1536, 256], P(('rep', 'yz', 'gx')), parts along dimension 0, may hold values from -6 to 6
- lengths: int32 [64], P(('rep', 'yz', 'gx')), parts along dimension 0, may hold values from 192 to 1536, as said below
Outputs:
- attended: bfloat16 [64, 3, 18432], P(('rep', 'yz'), None, 'gx'), parts along dimension 0
The draws below stay inside these ranges and needn't reach their ends.
There are 2 independent parts, one for each index of `rep`. The reference program is written for one: setup_inputs(seed, part) draws one part's arguments, and reference() takes and returns one part's arrays. A program takes and returns all parts, laid end to end along the dimension named above; an argument that names none is the same for every part. Nothing has to cross between parts.
Inputs may be any that keep to these rules, and one draw needn't show every extreme that they name: `lengths`: each row has at least 192 live cached positions; some row has all 1536.
All inputs are finite; a program needn't handle non-finite values.
Results may differ from the reference program's by a relative error of at most 0.014.
The reference program's roundings to bfloat16 on the way count: a program that leaves them out, or rounds other values in their place, can miss the bound.
Values may be sent and summed in bfloat16 or wider, within the bound.
A program may use at most 128 MiB of HBM per device.

```python
import math
import jax
import jax.numpy as jnp
from jax import lax

D = 18432
HD = 256
HEADS = 8
CACHE = 1536
STEPS = 3
ROWS = 32


def draw_key_cache(key, part):
    key = jax.random.fold_in(key, 11)
    first_key = jax.random.fold_in(key, 0)
    standard = jnp.clip(jax.random.normal(first_key, (ROWS, CACHE, HD), jnp.float32), -5.0, 5.0)
    return standard.astype(jnp.bfloat16)


def draw_lengths(key, part):
    key = jax.random.fold_in(key, 7)
    first_key, second_key = jax.random.split(key)
    drawn = jax.random.randint(first_key, (ROWS,), CACHE // 8, CACHE + 1, jnp.int32)
    chosen = jax.random.randint(second_key, (), 0, ROWS, jnp.int32)
    return jnp.where(jnp.arange(ROWS, dtype=jnp.int32) == chosen, jnp.int32(CACHE), drawn)


def levels(own_key, extent, cuts, smallest, largest):
    def one(dim, blocks):
        steps = jax.random.uniform(jax.random.fold_in(jax.random.fold_in(own_key, 6), dim), (blocks,), jnp.float32, smallest / len(cuts), largest / len(cuts))
        return jnp.repeat(jnp.exp(steps), extent[dim] // blocks).reshape((-1,) + (1,) * (len(extent) - dim - 1))

    loudness = one(*cuts[0])
    for cut in cuts[1:]:
        loudness = loudness * one(*cut)
    return loudness


def scatter_about(rng, dims, scale, bound, pieces=(), kind=jnp.bfloat16):
    gain = levels(rng, dims, pieces, -0.22, 0.18) if pieces else 1.0
    values = jax.random.normal(rng, dims, jnp.float32) * scale * gain
    return jnp.minimum(jnp.maximum(values, -bound), bound).astype(kind)


def setup_inputs(seed: int = 0, part: int = 0) -> dict:
    seeds = jax.random.split(jax.random.key(seed), 9)
    part_splits = jax.random.split(jax.random.fold_in(seeds[8], part), 9)
    return {
        "tokens": scatter_about(part_splits[0], (ROWS, STEPS, D), 1.0, 6.0, ((0, 8), (2, 2))),
        "query_weight": scatter_about(seeds[1], (D, HEADS * HD), D ** -0.5, 0.046875, ((0, 2), (1, 8))),
        "key_weight": scatter_about(seeds[2], (D, HD), (3.0 * D ** -0.5), 0.3125, ((0, 2), (1, 8))),
        "value_weight": scatter_about(seeds[3], (D, HD), D ** -0.5, 0.046875, ((0, 2), (1, 8))),
        "out_weight": scatter_about(seeds[4], (HEADS * HD, D), (HEADS * HD) ** -0.5, 0.125, ((0, 8), (1, 2))),
        "key_cache": draw_key_cache(jax.random.fold_in(jax.random.fold_in(seeds[8], part), 71), part),
        "value_cache": scatter_about(part_splits[6], (ROWS, CACHE, HD), 1.0, 6.0, ((0, 16),)),
        "lengths": draw_lengths(jax.random.fold_in(jax.random.fold_in(seeds[8], part), 71), part),
    }


def rotate(values, positions):
    half_dim = values.shape[-1] // 2
    frequency = jnp.exp(jnp.arange(half_dim, dtype=jnp.float32) * (-math.log(10000.0) / half_dim))
    angles = positions[..., None] * frequency
    cosine = jnp.cos(angles)
    sine_part = jnp.sin(angles)
    front_half = values[..., :half_dim]
    back_half = values[..., half_dim:]
    return jnp.concatenate([front_half * cosine - back_half * sine_part, back_half * cosine + front_half * sine_part], axis=-1)


def normalize(cache_scores, new_scores, lengths, steps_count):
    cache_len = cache_scores.shape[-1]
    cache_live = (jnp.arange(cache_len, dtype=jnp.int32)[None, :] < lengths[:, None])[:, None, None, :]
    new_live = (jnp.arange(steps_count, dtype=jnp.int32)[None, :] <= jnp.arange(steps_count, dtype=jnp.int32)[:, None])[None, :, None, :]
    floor_value = jnp.float32(-1e30)
    cache_scores = jnp.where(cache_live, cache_scores, floor_value)
    new_scores = jnp.where(new_live, new_scores, floor_value)
    highest = jnp.maximum(jnp.max(cache_scores, axis=-1, keepdims=True), jnp.max(new_scores, axis=-1, keepdims=True))
    cache_exp = jnp.exp(cache_scores - highest)
    new_exp = jnp.exp(new_scores - highest)
    denominator = jnp.sum(cache_exp, axis=-1, keepdims=True) + jnp.sum(new_exp, axis=-1, keepdims=True)
    return (cache_exp / denominator).astype(jnp.bfloat16), (new_exp / denominator).astype(jnp.bfloat16)


def reference(tokens, query_weight, key_weight, value_weight, out_weight, key_cache, value_cache, lengths):
    flattened = tokens.reshape(ROWS * STEPS, D)
    queries = jnp.dot(flattened, query_weight, preferred_element_type=jnp.float32).reshape(ROWS, STEPS, HEADS, HD)
    key_part = jnp.dot(flattened, key_weight, preferred_element_type=jnp.float32).reshape(ROWS, STEPS, HD)
    new_values = jnp.dot(flattened, value_weight, preferred_element_type=jnp.float32).reshape(ROWS, STEPS, HD).astype(jnp.bfloat16)
    positions = (lengths[:, None] + jnp.arange(STEPS, dtype=jnp.int32)[None, :]).astype(jnp.float32)
    rot_queries = rotate(queries, positions[:, :, None]).astype(jnp.bfloat16)
    new_keys = rotate(key_part, positions).astype(jnp.bfloat16)
    scale_factor = HD ** -0.5
    query_float = rot_queries.astype(jnp.float32)
    cache_scores = jnp.einsum("rshd,rkd->rshk", query_float, key_cache.astype(jnp.float32)) * scale_factor
    new_scores = jnp.einsum("rshd,rtd->rsht", query_float, new_keys.astype(jnp.float32)) * scale_factor
    cache_probs, new_probs = normalize(cache_scores, new_scores, lengths, STEPS)
    head_out = jnp.einsum("rshk,rkd->rshd", cache_probs.astype(jnp.float32), value_cache.astype(jnp.float32))
    head_out = head_out + jnp.einsum("rsht,rtd->rshd", new_probs.astype(jnp.float32), new_values.astype(jnp.float32))
    head_out = head_out.astype(jnp.bfloat16)
    heads_first = jnp.transpose(head_out, (2, 0, 1, 3)).reshape(HEADS, ROWS * STEPS, HD)
    weight_heads = out_weight.reshape(HEADS, HD, D)

    def add_head(running, paired):
        head_term = jnp.dot(paired[0], paired[1], preferred_element_type=jnp.float32).astype(jnp.bfloat16)
        head_term = lax.optimization_barrier(head_term)
        return running + head_term.astype(jnp.float32), None

    summed, unused = lax.scan(add_head, jnp.zeros((ROWS * STEPS, D), jnp.float32), (heads_first, weight_heads))
    return summed.astype(jnp.bfloat16).reshape(ROWS, STEPS, D)
```

```python
import math

import jax
import jax.numpy as jnp
from jax import lax
from jax.experimental import pallas as pl
from jax.experimental.pallas import tpu as pltpu
from jax.sharding import PartitionSpec as P

HD = 256
STEPS = 3


def rotate(values, positions):
    half_dim = values.shape[-1] // 2
    frequency = jnp.exp(jnp.arange(half_dim, dtype=jnp.float32) * (-math.log(10000.0) / half_dim))
    angles = positions[..., None] * frequency
    cosine = jnp.cos(angles)
    sine_part = jnp.sin(angles)
    front_half = values[..., :half_dim]
    back_half = values[..., half_dim:]
    return jnp.concatenate(
        [front_half * cosine - back_half * sine_part, back_half * cosine + front_half * sine_part],
        axis=-1,
    )


def normalize(cache_scores, new_scores, lengths, steps_count):
    cache_len = cache_scores.shape[-1]
    cache_live = (jnp.arange(cache_len, dtype=jnp.int32)[None, :] < lengths[:, None])[
        :, None, None, :
    ]
    new_live = (
        jnp.arange(steps_count, dtype=jnp.int32)[None, :]
        <= jnp.arange(steps_count, dtype=jnp.int32)[:, None]
    )[None, :, None, :]
    floor_value = jnp.float32(-1e30)
    cache_scores = jnp.where(cache_live, cache_scores, floor_value)
    new_scores = jnp.where(new_live, new_scores, floor_value)
    highest = jnp.maximum(
        jnp.max(cache_scores, axis=-1, keepdims=True), jnp.max(new_scores, axis=-1, keepdims=True)
    )
    cache_exp = jnp.exp(cache_scores - highest)
    new_exp = jnp.exp(new_scores - highest)
    denominator = jnp.sum(cache_exp, axis=-1, keepdims=True) + jnp.sum(
        new_exp, axis=-1, keepdims=True
    )
    return (
        (cache_exp / denominator).astype(jnp.bfloat16),
        (new_exp / denominator).astype(jnp.bfloat16),
    )


def local(
    tokens, query_weight, key_weight, value_weight, out_weight, key_cache, value_cache, lengths
):
    yz_count = lax.axis_size("yz")
    gx_count = lax.axis_size("gx")
    rows_here = lengths.shape[0]
    gathered = lax.all_gather(tokens, "yz", axis=0, tiled=True)
    all_rows = gathered.shape[0]
    flattened = gathered.reshape(all_rows * STEPS, gathered.shape[2])
    query_part = jnp.dot(flattened, query_weight, preferred_element_type=jnp.float32)
    key_part = jnp.dot(flattened, key_weight, preferred_element_type=jnp.float32)
    value_part = jnp.dot(flattened, value_weight, preferred_element_type=jnp.float32)
    arrived = (
        lax.all_to_all(
            query_part.reshape(yz_count * gx_count, rows_here, STEPS, 1, query_part.shape[1]),
            ("yz", "gx"),
            split_axis=0,
            concat_axis=3,
            tiled=True,
        ),
        lax.all_to_all(
            key_part.reshape(yz_count * gx_count, rows_here, STEPS, 1, key_part.shape[1]),
            ("yz", "gx"),
            split_axis=0,
            concat_axis=3,
            tiled=True,
        ),
        lax.all_to_all(
            value_part.reshape(yz_count * gx_count, rows_here, STEPS, 1, value_part.shape[1]),
            ("yz", "gx"),
            split_axis=0,
            concat_axis=3,
            tiled=True,
        ),
    )
    totals = [
        jnp.sum(member.reshape(rows_here, STEPS, yz_count, gx_count, member.shape[-1]), axis=3)
        for member in arrived
    ]
    queries = totals[0]
    key_sum = totals[1].reshape(rows_here, STEPS, HD)
    new_values = totals[2].reshape(rows_here, STEPS, HD).astype(jnp.bfloat16)
    positions = (lengths[:, None] + jnp.arange(STEPS, dtype=jnp.int32)[None, :]).astype(jnp.float32)
    rot_queries = rotate(queries, positions[:, :, None]).astype(jnp.bfloat16)
    new_keys = rotate(key_sum, positions).astype(jnp.bfloat16)
    scale_factor = HD ** (-0.5)
    cache_scores = (
        jnp.einsum("rshd,rkd->rshk", rot_queries, key_cache, preferred_element_type=jnp.float32)
        * scale_factor
    )
    new_scores = (
        jnp.einsum("rshd,rtd->rsht", rot_queries, new_keys, preferred_element_type=jnp.float32)
        * scale_factor
    )
    cache_probs, new_probs = normalize(cache_scores, new_scores, lengths, STEPS)
    head_out = jnp.einsum(
        "rshk,rkd->rshd", cache_probs, value_cache, preferred_element_type=jnp.float32
    )
    head_out = head_out + jnp.einsum(
        "rsht,rtd->rshd", new_probs, new_values, preferred_element_type=jnp.float32
    )
    head_out = head_out.astype(jnp.bfloat16)
    returned = lax.all_to_all(head_out, "yz", split_axis=2, concat_axis=0, tiled=True)
    paired = lax.all_gather(
        returned.reshape(yz_count, 1, rows_here, STEPS, HD), "gx", axis=1, tiled=True
    )
    head_rows = paired.reshape(all_rows, STEPS, HD)
    row_count = tokens.shape[0] * lax.axis_size("yz")
    product = jnp.dot(
        head_rows.reshape(row_count * STEPS, HD), out_weight, preferred_element_type=jnp.float32
    )
    return lax.psum_scatter(
        product.reshape(row_count, STEPS, out_weight.shape[1]).astype(jnp.bfloat16),
        "yz",
        scatter_dimension=0,
        tiled=True,
    )


FOLD = 4
CHUNKS = 3
NZ = 4
NY = 2
MESH = pl.DeviceIdType.MESH


def place():
    me = lax.axis_index("yz")
    return me // NY, me % NY


def greet(z, y):
    barrier = pltpu.get_barrier_semaphore()
    pl.semaphore_signal(barrier, inc=1, device_id={"yz": z * NY + 1 - y}, device_id_type=MESH)

    @pl.when(z > 0)
    def _():
        pl.semaphore_signal(barrier, inc=1, device_id={"yz": (z - 1) * NY + y}, device_id_type=MESH)

    @pl.when(z < NZ - 1)
    def _():
        pl.semaphore_signal(barrier, inc=1, device_id={"yz": (z + 1) * NY + y}, device_id_type=MESH)

    pl.semaphore_wait(barrier, jnp.where(jnp.logical_and(z > 0, z < NZ - 1), 3, 2))


def gather_project_kernel(
    tokens_ref, qw_ref, kw_ref, vw_ref, q_out, k_out, v_out,
    gathered, qw, kw, vw, w_sem, own_sem, up_send, down_send, side_send, recv,
):
    z, y = place()
    width = gathered.shape[3]
    rows = gathered.shape[2]
    features = qw.shape[0] // FOLD
    loads = [
        pltpu.make_async_copy(source, target, w_sem.at[i])
        for i, (source, target) in enumerate(((qw_ref, qw), (kw_ref, kw), (vw_ref, vw)))
    ]
    own = [
        pltpu.make_async_copy(
            tokens_ref.at[:, pl.ds(c * width, width)], gathered.at[c, z * NY + y], own_sem.at[c]
        )
        for c in range(CHUNKS)
    ]
    for copy in own:
        copy.start()
    greet(z, y)

    def block(c, origin_z, origin_y, target, sem):
        origin = origin_z * NY + origin_y
        return pltpu.make_async_remote_copy(
            src_ref=gathered.at[c, origin],
            dst_ref=gathered.at[c, origin],
            send_sem=sem.at[c, origin_z],
            recv_sem=recv.at[c, origin],
            device_id={"yz": target},
            device_id_type=MESH,
        )

    side = z * NY + 1 - y

    def up(c, origin_z):
        return block(c, origin_z, y, (z + 1) * NY + y, up_send)

    def down(c, origin_z):
        return block(c, origin_z, y, (z - 1) * NY + y, down_send)

    def across(c, origin_z):
        return block(c, origin_z, y, side, side_send)

    def arrival(c, origin_z, origin_y):
        block(c, origin_z, origin_y, side, side_send).wait_recv()

    for c in range(CHUNKS):
        own[c].wait()

        @pl.when(z < NZ - 1)
        def _(c=c):
            up(c, z).start()

        @pl.when(z > 0)
        def _(c=c):
            down(c, z).start()

        across(c, z).start()
    for copy in loads:
        copy.start()

    def forward(c):
        for k in range(1, NZ):
            @pl.when(z >= k)
            def _(k=k):
                arrival(c, z - k, y)

                @pl.when(z < NZ - 1)
                def _():
                    up(c, z - k).start()

                across(c, z - k).start()

            @pl.when(z + k < NZ)
            def _(k=k):
                arrival(c, z + k, y)

                @pl.when(z > 0)
                def _():
                    down(c, z + k).start()

                across(c, z + k).start()

    def multiply(c):
        for origin_z in range(NZ):
            arrival(c, origin_z, 1 - y)
        block_rows = gathered[c].reshape(NZ * NY * rows, width)
        fold = (lax.broadcasted_iota(jnp.int32, (NZ * NY * rows, 1), 0) % rows) // (rows // FOLD)
        for out, weight in ((q_out, qw), (k_out, kw), (v_out, vw)):
            total = None
            for f in range(FOLD):
                term = jnp.dot(
                    block_rows,
                    weight[pl.ds(f * features + c * width, width), :],
                    preferred_element_type=jnp.float32,
                )
                total = term if f == 0 else jnp.where(fold == f, term, total)
            if c == 0:
                out[...] = total
            else:
                out[...] += total

    for c in range(CHUNKS):
        forward(c)
        if c == 1:
            for copy in loads:
                copy.wait()
        if c > 0:
            multiply(c - 1)
    multiply(CHUNKS - 1)

    for c in range(CHUNKS):
        for origin_z in range(NZ):
            across(c, origin_z).wait_send()

            @pl.when(jnp.logical_and(z < NZ - 1, origin_z <= z))
            def _(c=c, origin_z=origin_z):
                up(c, origin_z).wait_send()

            @pl.when(jnp.logical_and(z > 0, origin_z >= z))
            def _(c=c, origin_z=origin_z):
                down(c, origin_z).wait_send()


def gather_project(folded, query_weight, key_weight, value_weight):
    rows, features = folded.shape
    width = features // CHUNKS
    count = NZ * NY
    outs = [w.shape[1] for w in (query_weight, key_weight, value_weight)]
    hbm = pl.BlockSpec(memory_space=pl.ANY)
    vmem = pl.BlockSpec(memory_space=pltpu.VMEM)
    dma = pltpu.SemaphoreType.DMA
    return pl.pallas_call(
        gather_project_kernel,
        out_shape=[jax.ShapeDtypeStruct((count * rows, n), jnp.float32) for n in outs],
        in_specs=[hbm] * 4,
        out_specs=[vmem] * 3,
        scratch_shapes=[
            pltpu.VMEM((CHUNKS, count, rows, width), jnp.bfloat16),
            pltpu.VMEM(query_weight.shape, jnp.bfloat16),
            pltpu.VMEM(key_weight.shape, jnp.bfloat16),
            pltpu.VMEM(value_weight.shape, jnp.bfloat16),
            dma((3,)),
            dma((CHUNKS,)),
            dma((CHUNKS, NZ)),
            dma((CHUNKS, NZ)),
            dma((CHUNKS, NZ)),
            dma((CHUNKS, count)),
        ],
        compiler_params=pltpu.CompilerParams(
            collective_id=0, has_side_effects=True, vmem_limit_bytes=48 * 1024 * 1024
        ),
        name="gather_project",
    )(folded, query_weight, key_weight, value_weight)


def project_scatter_kernel(
    heads_ref, weight_ref, out_ref,
    weight, terms, side_in, up_in, down_in,
    w_sem, side_send, side_recv, line_send, up_recv, down_recv,
):
    z, y = place()
    rows, width = terms.shape[2], terms.shape[3]
    depth = weight_ref.shape[0]
    features = weight_ref.shape[1] // FOLD
    loads = [
        [
            pltpu.make_async_copy(
                weight_ref.at[:, pl.ds(f * features + c * width, width)],
                weight.at[c, pl.ds(f * depth, depth), :],
                w_sem.at[c, f],
            )
            for f in range(FOLD)
        ]
        for c in range(CHUNKS)
    ]
    for group in loads:
        for copy in group:
            copy.start()
    greet(z, y)

    def across(c, dest):
        return pltpu.make_async_remote_copy(
            src_ref=terms.at[c, dest * NY + 1 - y],
            dst_ref=side_in.at[c, dest],
            send_sem=side_send.at[c, dest],
            recv_sem=side_recv.at[c, dest],
            device_id={"yz": z * NY + 1 - y},
            device_id_type=MESH,
        )

    def along(c, dest, step):
        return pltpu.make_async_remote_copy(
            src_ref=terms.at[c, dest * NY + y],
            dst_ref=(up_in if step > 0 else down_in).at[c, dest],
            send_sem=line_send.at[c, dest],
            recv_sem=(up_recv if step > 0 else down_recv).at[c, dest],
            device_id={"yz": (z + step) * NY + y},
            device_id_type=MESH,
        )

    for c in range(CHUNKS):
        for copy in loads[c]:
            copy.wait()
        product = jnp.dot(heads_ref[...], weight[c], preferred_element_type=jnp.float32)
        terms[c] = product.astype(jnp.bfloat16).reshape(NZ * NY, rows, width)
        for k in range(NZ - 1, 0, -1):
            @pl.when(z + k < NZ)
            def _(c=c, k=k):
                across(c, z + k).start()

            @pl.when(z >= k)
            def _(c=c, k=k):
                across(c, z - k).start()

        across(c, z).start()

    def own_pair(c, dest):
        across(c, dest).wait_recv()
        return terms[c, dest * NY + y].astype(jnp.float32) + side_in[c, dest].astype(jnp.float32)

    def pass_on(c, dest, step, has_source):
        arrived = up_in if step > 0 else down_in
        total = own_pair(c, dest)
        terms[c, dest * NY + y] = total.astype(jnp.bfloat16)

        @pl.when(has_source)
        def _():
            along(c, dest, step).wait_recv()
            terms[c, dest * NY + y] = (total + arrived[c, dest].astype(jnp.float32)).astype(
                jnp.bfloat16
            )

        along(c, dest, step).start()

    for c in range(CHUNKS):
        for k in range(NZ - 1, 0, -1):
            @pl.when(z + k < NZ)
            def _(c=c, k=k):
                pass_on(c, z + k, 1, z > 0)

            @pl.when(z >= k)
            def _(c=c, k=k):
                pass_on(c, z - k, -1, z < NZ - 1)

        here = pl.ds(c * width, width)
        total = own_pair(c, z)

        @pl.when(z == 0)
        def _(c=c, here=here, total=total):
            along(c, z, -1).wait_recv()
            out_ref[:, here] = (total + down_in[c, z].astype(jnp.float32)).astype(jnp.bfloat16)

        @pl.when(z == NZ - 1)
        def _(c=c, here=here, total=total):
            along(c, z, 1).wait_recv()
            out_ref[:, here] = (total + up_in[c, z].astype(jnp.float32)).astype(jnp.bfloat16)

        @pl.when(jnp.logical_and(z > 0, z < NZ - 1))
        def _(c=c, here=here, total=total):
            along(c, z, 1).wait_recv()
            along(c, z, -1).wait_recv()
            out_ref[:, here] = (
                total + up_in[c, z].astype(jnp.float32) + down_in[c, z].astype(jnp.float32)
            ).astype(jnp.bfloat16)

    for c in range(CHUNKS):
        for dest in range(NZ):
            across(c, dest).wait_send()

            @pl.when(dest != z)
            def _(c=c, dest=dest):
                along(c, dest, 1).wait_send()


def project_scatter(heads, out_weight):
    depth, columns = out_weight.shape
    count = NZ * NY
    rows = heads.shape[0] // count
    width = columns // FOLD // CHUNKS
    dma = pltpu.SemaphoreType.DMA
    vmem = pl.BlockSpec(memory_space=pltpu.VMEM)
    landing = pltpu.VMEM((CHUNKS, NZ, rows, width), jnp.bfloat16)
    sems = dma((CHUNKS, NZ))
    return pl.pallas_call(
        project_scatter_kernel,
        out_shape=jax.ShapeDtypeStruct((rows, columns // FOLD), jnp.bfloat16),
        in_specs=[vmem, pl.BlockSpec(memory_space=pl.ANY)],
        out_specs=vmem,
        scratch_shapes=[
            pltpu.VMEM((CHUNKS, FOLD * depth, width), jnp.bfloat16),
            pltpu.VMEM((CHUNKS, count, rows, width), jnp.bfloat16),
            landing,
            landing,
            landing,
            dma((CHUNKS, FOLD)),
            sems,
            sems,
            sems,
            sems,
            sems,
        ],
        compiler_params=pltpu.CompilerParams(
            collective_id=1, has_side_effects=True, vmem_limit_bytes=48 * 1024 * 1024
        ),
        name="project_scatter",
    )(heads, out_weight)


def attend(queries, key_sum, new_values, key_cache, value_cache, lengths):
    positions = (lengths[:, None] + jnp.arange(STEPS, dtype=jnp.int32)[None, :]).astype(jnp.float32)
    rot_queries = rotate(queries, positions[:, :, None]).astype(jnp.bfloat16)
    new_keys = rotate(key_sum, positions).astype(jnp.bfloat16)
    scale_factor = HD ** (-0.5)
    cache_scores = (
        jnp.einsum("rshd,rkd->rshk", rot_queries, key_cache, preferred_element_type=jnp.float32)
        * scale_factor
    )
    new_scores = (
        jnp.einsum("rshd,rtd->rsht", rot_queries, new_keys, preferred_element_type=jnp.float32)
        * scale_factor
    )
    cache_probs, new_probs = normalize(cache_scores, new_scores, lengths, STEPS)
    head_out = jnp.einsum(
        "rshk,rkd->rshd", cache_probs, value_cache, preferred_element_type=jnp.float32
    )
    head_out = head_out + jnp.einsum(
        "rsht,rtd->rshd", new_probs, new_values, preferred_element_type=jnp.float32
    )
    return head_out.astype(jnp.bfloat16)


def local_line(
    tokens, query_weight, key_weight, value_weight, out_weight, key_cache, value_cache, lengths
):
    yz_count = lax.axis_size("yz")
    gx_count = lax.axis_size("gx")
    rows_here = lengths.shape[0]
    owned = tokens.shape[0] * STEPS
    features = tokens.shape[2]
    folded = (
        tokens.reshape(owned, FOLD, features // FOLD)
        .transpose(1, 0, 2)
        .reshape(FOLD * owned, features // FOLD)
    )
    parts = gather_project(folded, query_weight, key_weight, value_weight)
    joined = jnp.concatenate(parts, axis=1)
    joined = joined.reshape(yz_count, FOLD, owned, joined.shape[1]).sum(axis=1)
    arrived = lax.all_to_all(
        joined.reshape(yz_count * gx_count, rows_here * STEPS, joined.shape[-1]),
        ("yz", "gx"),
        split_axis=0,
        concat_axis=0,
        tiled=True,
    )
    totals = arrived.reshape(yz_count, gx_count, rows_here, STEPS, -1).sum(axis=1)
    totals = totals.transpose(1, 2, 0, 3)
    key_columns = key_weight.shape[1]
    queries = totals[..., :HD]
    key_sum = totals[..., HD : HD + key_columns].reshape(rows_here, STEPS, HD)
    new_values = totals[..., HD + key_columns :].reshape(rows_here, STEPS, HD).astype(jnp.bfloat16)
    head_out = attend(queries, key_sum, new_values, key_cache, value_cache, lengths)
    by_head = head_out.reshape(rows_here * STEPS, yz_count, HD).transpose(1, 0, 2)
    sent = jnp.broadcast_to(by_head[:, None], (yz_count, gx_count) + by_head.shape[1:])
    returned = lax.all_to_all(
        sent.reshape(yz_count * gx_count, rows_here * STEPS, HD),
        ("yz", "gx"),
        split_axis=0,
        concat_axis=0,
        tiled=True,
    )
    heads = returned.reshape(yz_count, 1, owned, 1, HD)
    same = jnp.eye(FOLD, dtype=bool)[None, :, None, :, None]
    heads = jnp.where(same, heads, jnp.bfloat16(0)).reshape(yz_count * FOLD * owned, FOLD * HD)
    summed = project_scatter(heads, out_weight)
    return (
        summed.reshape(FOLD, owned, -1).transpose(1, 0, 2).reshape(tokens.shape[0], STEPS, features)
    )


def solution(mesh):
    body = local_line if mesh.shape["yz"] == NZ * NY and mesh.shape["gx"] == 2 else local
    placed = (
        P(("rep", "yz"), None, "gx"),
        P("gx", "yz"),
        P("gx", "yz"),
        P("gx", "yz"),
        P("yz", "gx"),
        P(("rep", "yz", "gx"), None, None),
        P(("rep", "yz", "gx"), None, None),
        P(("rep", "yz", "gx")),
    )
    return jax.shard_map(
        body, mesh=mesh, in_specs=placed, out_specs=P(("rep", "yz"), None, "gx"), check_vma=False
    )
```

```python
import math

import jax
import jax.numpy as jnp
from jax import lax
from jax.experimental import pallas as pl
from jax.experimental.pallas import tpu as pltpu
from jax.sharding import PartitionSpec as P

HD = 256
STEPS = 3


def rotate(values, positions):
    half_dim = values.shape[-1] // 2
    frequency = jnp.exp(jnp.arange(half_dim, dtype=jnp.float32) * (-math.log(10000.0) / half_dim))
    angles = positions[..., None] * frequency
    cosine = jnp.cos(angles)
    sine_part = jnp.sin(angles)
    front_half = values[..., :half_dim]
    back_half = values[..., half_dim:]
    return jnp.concatenate(
        [front_half * cosine - back_half * sine_part, back_half * cosine + front_half * sine_part],
        axis=-1,
    )


def normalize(cache_scores, new_scores, lengths, steps_count):
    cache_len = cache_scores.shape[-1]
    cache_live = (jnp.arange(cache_len, dtype=jnp.int32)[None, :] < lengths[:, None])[
        :, None, None, :
    ]
    new_live = (
        jnp.arange(steps_count, dtype=jnp.int32)[None, :]
        <= jnp.arange(steps_count, dtype=jnp.int32)[:, None]
    )[None, :, None, :]
    floor_value = jnp.float32(-1e30)
    cache_scores = jnp.where(cache_live, cache_scores, floor_value)
    new_scores = jnp.where(new_live, new_scores, floor_value)
    highest = jnp.maximum(
        jnp.max(cache_scores, axis=-1, keepdims=True), jnp.max(new_scores, axis=-1, keepdims=True)
    )
    cache_exp = jnp.exp(cache_scores - highest)
    new_exp = jnp.exp(new_scores - highest)
    denominator = jnp.sum(cache_exp, axis=-1, keepdims=True) + jnp.sum(
        new_exp, axis=-1, keepdims=True
    )
    return (
        (cache_exp / denominator).astype(jnp.bfloat16),
        (new_exp / denominator).astype(jnp.bfloat16),
    )


def local(
    tokens, query_weight, key_weight, value_weight, out_weight, key_cache, value_cache, lengths
):
    yz_count = lax.axis_size("yz")
    gx_count = lax.axis_size("gx")
    rows_here = lengths.shape[0]
    gathered = lax.all_gather(tokens, "yz", axis=0, tiled=True)
    all_rows = gathered.shape[0]
    flattened = gathered.reshape(all_rows * STEPS, gathered.shape[2])
    query_part = jnp.dot(flattened, query_weight, preferred_element_type=jnp.float32)
    key_part = jnp.dot(flattened, key_weight, preferred_element_type=jnp.float32)
    value_part = jnp.dot(flattened, value_weight, preferred_element_type=jnp.float32)
    arrived = (
        lax.all_to_all(
            query_part.reshape(yz_count * gx_count, rows_here, STEPS, 1, query_part.shape[1]),
            ("yz", "gx"),
            split_axis=0,
            concat_axis=3,
            tiled=True,
        ),
        lax.all_to_all(
            key_part.reshape(yz_count * gx_count, rows_here, STEPS, 1, key_part.shape[1]),
            ("yz", "gx"),
            split_axis=0,
            concat_axis=3,
            tiled=True,
        ),
        lax.all_to_all(
            value_part.reshape(yz_count * gx_count, rows_here, STEPS, 1, value_part.shape[1]),
            ("yz", "gx"),
            split_axis=0,
            concat_axis=3,
            tiled=True,
        ),
    )
    totals = [
        jnp.sum(member.reshape(rows_here, STEPS, yz_count, gx_count, member.shape[-1]), axis=3)
        for member in arrived
    ]
    queries = totals[0]
    key_sum = totals[1].reshape(rows_here, STEPS, HD)
    new_values = totals[2].reshape(rows_here, STEPS, HD).astype(jnp.bfloat16)
    positions = (lengths[:, None] + jnp.arange(STEPS, dtype=jnp.int32)[None, :]).astype(jnp.float32)
    rot_queries = rotate(queries, positions[:, :, None]).astype(jnp.bfloat16)
    new_keys = rotate(key_sum, positions).astype(jnp.bfloat16)
    scale_factor = HD ** (-0.5)
    cache_scores = (
        jnp.einsum("rshd,rkd->rshk", rot_queries, key_cache, preferred_element_type=jnp.float32)
        * scale_factor
    )
    new_scores = (
        jnp.einsum("rshd,rtd->rsht", rot_queries, new_keys, preferred_element_type=jnp.float32)
        * scale_factor
    )
    cache_probs, new_probs = normalize(cache_scores, new_scores, lengths, STEPS)
    head_out = jnp.einsum(
        "rshk,rkd->rshd", cache_probs, value_cache, preferred_element_type=jnp.float32
    )
    head_out = head_out + jnp.einsum(
        "rsht,rtd->rshd", new_probs, new_values, preferred_element_type=jnp.float32
    )
    head_out = head_out.astype(jnp.bfloat16)
    returned = lax.all_to_all(head_out, "yz", split_axis=2, concat_axis=0, tiled=True)
    paired = lax.all_gather(
        returned.reshape(yz_count, 1, rows_here, STEPS, HD), "gx", axis=1, tiled=True
    )
    head_rows = paired.reshape(all_rows, STEPS, HD)
    row_count = tokens.shape[0] * lax.axis_size("yz")
    product = jnp.dot(
        head_rows.reshape(row_count * STEPS, HD), out_weight, preferred_element_type=jnp.float32
    )
    return lax.psum_scatter(
        product.reshape(row_count, STEPS, out_weight.shape[1]).astype(jnp.bfloat16),
        "yz",
        scatter_dimension=0,
        tiled=True,
    )


FOLD = 4
CHUNKS = 3
AHEAD = 3
NZ = 4
NY = 2
MESH = pl.DeviceIdType.MESH


def place():
    me = lax.axis_index("yz")
    return me // NY, me % NY


def greet(z, y):
    barrier = pltpu.get_barrier_semaphore()
    pl.semaphore_signal(barrier, inc=1, device_id={"yz": z * NY + 1 - y}, device_id_type=MESH)

    @pl.when(z > 0)
    def _():
        pl.semaphore_signal(barrier, inc=1, device_id={"yz": (z - 1) * NY + y}, device_id_type=MESH)

    @pl.when(z < NZ - 1)
    def _():
        pl.semaphore_signal(barrier, inc=1, device_id={"yz": (z + 1) * NY + y}, device_id_type=MESH)

    pl.semaphore_wait(barrier, jnp.where(jnp.logical_and(z > 0, z < NZ - 1), 3, 2))


def gather_project_kernel(
    tokens_ref, qw_ref, kw_ref, vw_ref, q_out, kv_out,
    gathered, qw, kvw, w_sem, own_sem, up_send, down_send, side_send, recv,
):
    z, y = place()
    width = gathered.shape[3]
    rows = gathered.shape[2]
    features = qw.shape[0] // FOLD
    loads = [
        pltpu.make_async_copy(source, target, w_sem.at[i])
        for i, (source, target) in enumerate(
            (
                (qw_ref, qw),
                (kw_ref, kvw.at[pl.ds(0, kw_ref.shape[0]), :]),
                (vw_ref, kvw.at[pl.ds(kw_ref.shape[0], vw_ref.shape[0]), :]),
            )
        )
    ]
    own = [
        pltpu.make_async_copy(
            tokens_ref.at[:, pl.ds(c * width, width)], gathered.at[c, z * NY + y], own_sem.at[c]
        )
        for c in range(CHUNKS)
    ]
    for copy in own:
        copy.start()
    greet(z, y)

    def block(c, origin_z, origin_y, target, sem):
        origin = origin_z * NY + origin_y
        return pltpu.make_async_remote_copy(
            src_ref=gathered.at[c, origin],
            dst_ref=gathered.at[c, origin],
            send_sem=sem.at[c, origin_z],
            recv_sem=recv.at[c, origin],
            device_id={"yz": target},
            device_id_type=MESH,
        )

    side = z * NY + 1 - y

    def up(c, origin_z):
        return block(c, origin_z, y, (z + 1) * NY + y, up_send)

    def down(c, origin_z):
        return block(c, origin_z, y, (z - 1) * NY + y, down_send)

    def across(c, origin_z):
        return block(c, origin_z, y, side, side_send)

    def arrival(c, origin_z, origin_y):
        block(c, origin_z, origin_y, side, side_send).wait_recv()

    for c in range(CHUNKS):
        own[c].wait()

        @pl.when(z < NZ - 1)
        def _(c=c):
            up(c, z).start()

        @pl.when(z > 0)
        def _(c=c):
            down(c, z).start()

        across(c, z).start()
    for copy in loads:
        copy.start()

    def forward(c):
        for k in range(1, NZ):
            @pl.when(z >= k)
            def _(k=k):
                arrival(c, z - k, y)

                @pl.when(z < NZ - 1)
                def _():
                    up(c, z - k).start()

                across(c, z - k).start()

            @pl.when(z + k < NZ)
            def _(k=k):
                arrival(c, z + k, y)

                @pl.when(z > 0)
                def _():
                    down(c, z + k).start()

                across(c, z + k).start()

    def multiply(c):
        for origin_z in range(NZ):
            arrival(c, origin_z, 1 - y)
        block_rows = gathered[c].reshape(NZ * NY * rows, width)
        fold = (lax.broadcasted_iota(jnp.int32, (NZ * NY * rows, 1), 0) % rows) // (rows // FOLD)
        def project(out, weigh):
            total = None
            for f in range(FOLD):
                term = weigh(pl.ds(f * features + c * width, width))
                total = term if f == 0 else jnp.where(fold == f, term, total)
            if c == 0:
                out[...] = total
            else:
                out[...] += total

        project(
            q_out,
            lambda at: jnp.dot(block_rows, qw[at, :], preferred_element_type=jnp.float32),
        )
        project(
            kv_out,
            lambda at: lax.dot_general(
                block_rows, kvw[:, at], (((1,), (1,)), ((), ())), preferred_element_type=jnp.float32
            ),
        )

    for c in range(CHUNKS):
        forward(c)
        if c == 1:
            for copy in loads:
                copy.wait()
        if c > 0:
            multiply(c - 1)
    multiply(CHUNKS - 1)

    for c in range(CHUNKS):
        for origin_z in range(NZ):
            across(c, origin_z).wait_send()

            @pl.when(jnp.logical_and(z < NZ - 1, origin_z <= z))
            def _(c=c, origin_z=origin_z):
                up(c, origin_z).wait_send()

            @pl.when(jnp.logical_and(z > 0, origin_z >= z))
            def _(c=c, origin_z=origin_z):
                down(c, origin_z).wait_send()


def gather_project(folded, query_weight, key_weight, value_weight):
    rows, features = folded.shape
    width = features // CHUNKS
    count = NZ * NY
    outs = [query_weight.shape[1], key_weight.shape[1] + value_weight.shape[1]]
    hbm = pl.BlockSpec(memory_space=pl.ANY)
    vmem = pl.BlockSpec(memory_space=pltpu.VMEM)
    dma = pltpu.SemaphoreType.DMA
    return pl.pallas_call(
        gather_project_kernel,
        out_shape=[jax.ShapeDtypeStruct((count * rows, n), jnp.float32) for n in outs],
        in_specs=[hbm] * 4,
        out_specs=[vmem] * 2,
        scratch_shapes=[
            pltpu.VMEM((CHUNKS, count, rows, width), jnp.bfloat16),
            pltpu.VMEM(query_weight.shape, jnp.bfloat16),
            pltpu.VMEM((outs[1], query_weight.shape[0]), jnp.bfloat16),
            dma((3,)),
            dma((CHUNKS,)),
            dma((CHUNKS, NZ)),
            dma((CHUNKS, NZ)),
            dma((CHUNKS, NZ)),
            dma((CHUNKS, count)),
        ],
        compiler_params=pltpu.CompilerParams(
            collective_id=0, has_side_effects=True, vmem_limit_bytes=48 * 1024 * 1024
        ),
        name="gather_project",
    )(folded, query_weight, key_weight.T, value_weight.T)


def project_scatter_kernel(
    heads_ref, weight_ref, out_ref,
    weight, terms, side_in, up_in, down_in,
    w_sem, side_send, side_recv, line_send, up_recv, down_recv,
):
    z, y = place()
    rows, width = terms.shape[2], terms.shape[3]
    depth = weight_ref.shape[0]
    features = weight_ref.shape[1] // FOLD
    loads = [
        [
            pltpu.make_async_copy(
                weight_ref.at[:, pl.ds(f * features + c * width, width)],
                weight.at[c, pl.ds(f * depth, depth), :],
                w_sem.at[c, f],
            )
            for f in range(FOLD)
        ]
        for c in range(CHUNKS)
    ]
    for group in loads:
        for copy in group:
            copy.start()
    greet(z, y)

    def across(c, dest):
        return pltpu.make_async_remote_copy(
            src_ref=terms.at[c, dest * NY + 1 - y],
            dst_ref=side_in.at[c, dest],
            send_sem=side_send.at[c, dest],
            recv_sem=side_recv.at[c, dest],
            device_id={"yz": z * NY + 1 - y},
            device_id_type=MESH,
        )

    def along(c, dest, step):
        return pltpu.make_async_remote_copy(
            src_ref=terms.at[c, dest * NY + y],
            dst_ref=(up_in if step > 0 else down_in).at[c, dest],
            send_sem=line_send.at[c, dest],
            recv_sem=(up_recv if step > 0 else down_recv).at[c, dest],
            device_id={"yz": (z + step) * NY + y},
            device_id_type=MESH,
        )

    def multiply(c):
        for copy in loads[c]:
            copy.wait()
        product = jnp.dot(heads_ref[...], weight[c], preferred_element_type=jnp.float32)
        terms[c] = product.astype(jnp.bfloat16).reshape(NZ * NY, rows, width)

    def each_side(group, act):
        c, k = group // NZ, NZ - 1 - group % NZ
        if k == 0:
            act(across(c, z))
            return

        @pl.when(z + k < NZ)
        def _():
            act(across(c, z + k))

        @pl.when(z >= k)
        def _():
            act(across(c, z - k))

    def start_side(group):
        if group < CHUNKS * NZ:
            if group % NZ == 0:
                multiply(group // NZ)
            each_side(group, lambda copy: copy.start())

    for group in range(AHEAD):
        start_side(group)

    def own_pair(c, dest):
        across(c, dest).wait_recv()
        return terms[c, dest * NY + y].astype(jnp.float32) + side_in[c, dest].astype(jnp.float32)

    def pass_on(c, dest, step, has_source):
        arrived = up_in if step > 0 else down_in
        total = own_pair(c, dest)
        terms[c, dest * NY + y] = total.astype(jnp.bfloat16)

        @pl.when(has_source)
        def _():
            along(c, dest, step).wait_recv()
            terms[c, dest * NY + y] = (total + arrived[c, dest].astype(jnp.float32)).astype(
                jnp.bfloat16
            )

        along(c, dest, step).start()

    for c in range(CHUNKS):
        for k in range(NZ - 1, -1, -1):
            group = c * NZ + NZ - 1 - k
            each_side(group, lambda copy: copy.wait_send())
            start_side(group + AHEAD)
            if k == 0:
                break

            @pl.when(z + k < NZ)
            def _(c=c, k=k):
                pass_on(c, z + k, 1, z > 0)

            @pl.when(z >= k)
            def _(c=c, k=k):
                pass_on(c, z - k, -1, z < NZ - 1)

        here = pl.ds(c * width, width)
        total = own_pair(c, z)

        @pl.when(z == 0)
        def _(c=c, here=here, total=total):
            along(c, z, -1).wait_recv()
            out_ref[:, here] = (total + down_in[c, z].astype(jnp.float32)).astype(jnp.bfloat16)

        @pl.when(z == NZ - 1)
        def _(c=c, here=here, total=total):
            along(c, z, 1).wait_recv()
            out_ref[:, here] = (total + up_in[c, z].astype(jnp.float32)).astype(jnp.bfloat16)

        @pl.when(jnp.logical_and(z > 0, z < NZ - 1))
        def _(c=c, here=here, total=total):
            along(c, z, 1).wait_recv()
            along(c, z, -1).wait_recv()
            out_ref[:, here] = (
                total + up_in[c, z].astype(jnp.float32) + down_in[c, z].astype(jnp.float32)
            ).astype(jnp.bfloat16)

    for c in range(CHUNKS):
        for dest in range(NZ):
            @pl.when(dest != z)
            def _(c=c, dest=dest):
                along(c, dest, 1).wait_send()


def project_scatter(heads, out_weight):
    depth, columns = out_weight.shape
    count = NZ * NY
    rows = heads.shape[0] // count
    width = columns // FOLD // CHUNKS
    dma = pltpu.SemaphoreType.DMA
    vmem = pl.BlockSpec(memory_space=pltpu.VMEM)
    landing = pltpu.VMEM((CHUNKS, NZ, rows, width), jnp.bfloat16)
    sems = dma((CHUNKS, NZ))
    return pl.pallas_call(
        project_scatter_kernel,
        out_shape=jax.ShapeDtypeStruct((rows, columns // FOLD), jnp.bfloat16),
        in_specs=[vmem, pl.BlockSpec(memory_space=pl.ANY)],
        out_specs=vmem,
        scratch_shapes=[
            pltpu.VMEM((CHUNKS, FOLD * depth, width), jnp.bfloat16),
            pltpu.VMEM((CHUNKS, count, rows, width), jnp.bfloat16),
            landing,
            landing,
            landing,
            dma((CHUNKS, FOLD)),
            sems,
            sems,
            sems,
            sems,
            sems,
        ],
        compiler_params=pltpu.CompilerParams(
            collective_id=1, has_side_effects=True, vmem_limit_bytes=48 * 1024 * 1024
        ),
        name="project_scatter",
    )(heads, out_weight)


def attend(queries, key_sum, new_values, key_cache, value_cache, lengths):
    positions = (lengths[:, None] + jnp.arange(STEPS, dtype=jnp.int32)[None, :]).astype(jnp.float32)
    rot_queries = rotate(queries, positions[:, :, None]).astype(jnp.bfloat16)
    new_keys = rotate(key_sum, positions).astype(jnp.bfloat16)
    scale_factor = HD ** (-0.5)
    cache_scores = (
        jnp.einsum("rshd,rkd->rshk", rot_queries, key_cache, preferred_element_type=jnp.float32)
        * scale_factor
    )
    new_scores = (
        jnp.einsum("rshd,rtd->rsht", rot_queries, new_keys, preferred_element_type=jnp.float32)
        * scale_factor
    )
    cache_probs, new_probs = normalize(cache_scores, new_scores, lengths, STEPS)
    head_out = jnp.einsum(
        "rshk,rkd->rshd", cache_probs, value_cache, preferred_element_type=jnp.float32
    )
    head_out = head_out + jnp.einsum(
        "rsht,rtd->rshd", new_probs, new_values, preferred_element_type=jnp.float32
    )
    return head_out.astype(jnp.bfloat16)


def local_line(
    tokens, query_weight, key_weight, value_weight, out_weight, key_cache, value_cache, lengths
):
    yz_count = lax.axis_size("yz")
    gx_count = lax.axis_size("gx")
    rows_here = lengths.shape[0]
    owned = tokens.shape[0] * STEPS
    features = tokens.shape[2]
    folded = (
        tokens.reshape(owned, FOLD, features // FOLD)
        .transpose(1, 0, 2)
        .reshape(FOLD * owned, features // FOLD)
    )
    parts = gather_project(folded, query_weight, key_weight, value_weight)
    joined = jnp.concatenate(parts, axis=1)
    joined = joined.reshape(yz_count, FOLD, owned, joined.shape[1]).sum(axis=1)
    arrived = lax.all_to_all(
        joined.reshape(yz_count * gx_count, rows_here * STEPS, joined.shape[-1]),
        ("yz", "gx"),
        split_axis=0,
        concat_axis=0,
        tiled=True,
    )
    totals = arrived.reshape(yz_count, gx_count, rows_here, STEPS, -1).sum(axis=1)
    totals = totals.transpose(1, 2, 0, 3)
    key_columns = key_weight.shape[1]
    queries = totals[..., :HD]
    key_sum = totals[..., HD : HD + key_columns].reshape(rows_here, STEPS, HD)
    new_values = totals[..., HD + key_columns :].reshape(rows_here, STEPS, HD).astype(jnp.bfloat16)
    head_out = attend(queries, key_sum, new_values, key_cache, value_cache, lengths)
    by_head = head_out.reshape(rows_here * STEPS, yz_count, HD).transpose(1, 0, 2)
    sent = jnp.broadcast_to(by_head[:, None], (yz_count, gx_count) + by_head.shape[1:])
    returned = lax.all_to_all(
        sent.reshape(yz_count * gx_count, rows_here * STEPS, HD),
        ("yz", "gx"),
        split_axis=0,
        concat_axis=0,
        tiled=True,
    )
    heads = returned.reshape(yz_count, 1, owned, 1, HD)
    same = jnp.eye(FOLD, dtype=bool)[None, :, None, :, None]
    heads = jnp.where(same, heads, jnp.bfloat16(0)).reshape(yz_count * FOLD * owned, FOLD * HD)
    summed = project_scatter(heads, out_weight)
    return (
        summed.reshape(FOLD, owned, -1).transpose(1, 0, 2).reshape(tokens.shape[0], STEPS, features)
    )


def solution(mesh):
    body = local_line if mesh.shape["yz"] == NZ * NY and mesh.shape["gx"] == 2 else local
    placed = (
        P(("rep", "yz"), None, "gx"),
        P("gx", "yz"),
        P("gx", "yz"),
        P("gx", "yz"),
        P("yz", "gx"),
        P(("rep", "yz", "gx"), None, None),
        P(("rep", "yz", "gx"), None, None),
        P(("rep", "yz", "gx")),
    )
    return jax.shard_map(
        body, mesh=mesh, in_specs=placed, out_specs=P(("rep", "yz"), None, "gx"), check_vma=False
    )
```

```python
import math

import jax
import jax.numpy as jnp
from jax import lax
from jax.experimental import pallas as pl
from jax.experimental.pallas import tpu as pltpu
from jax.sharding import PartitionSpec as P

HD = 256
STEPS = 3


def rotate(values, positions):
    half_dim = values.shape[-1] // 2
    frequency = jnp.exp(jnp.arange(half_dim, dtype=jnp.float32) * (-math.log(10000.0) / half_dim))
    angles = positions[..., None] * frequency
    cosine = jnp.cos(angles)
    sine_part = jnp.sin(angles)
    front_half = values[..., :half_dim]
    back_half = values[..., half_dim:]
    return jnp.concatenate(
        [front_half * cosine - back_half * sine_part, back_half * cosine + front_half * sine_part],
        axis=-1,
    )


def normalize(cache_scores, new_scores, lengths, steps_count):
    cache_len = cache_scores.shape[-1]
    cache_live = (jnp.arange(cache_len, dtype=jnp.int32)[None, :] < lengths[:, None])[
        :, None, None, :
    ]
    new_live = (
        jnp.arange(steps_count, dtype=jnp.int32)[None, :]
        <= jnp.arange(steps_count, dtype=jnp.int32)[:, None]
    )[None, :, None, :]
    floor_value = jnp.float32(-1e30)
    cache_scores = jnp.where(cache_live, cache_scores, floor_value)
    new_scores = jnp.where(new_live, new_scores, floor_value)
    highest = jnp.maximum(
        jnp.max(cache_scores, axis=-1, keepdims=True), jnp.max(new_scores, axis=-1, keepdims=True)
    )
    cache_exp = jnp.exp(cache_scores - highest)
    new_exp = jnp.exp(new_scores - highest)
    denominator = jnp.sum(cache_exp, axis=-1, keepdims=True) + jnp.sum(
        new_exp, axis=-1, keepdims=True
    )
    return (
        (cache_exp / denominator).astype(jnp.bfloat16),
        (new_exp / denominator).astype(jnp.bfloat16),
    )


def local(
    tokens, query_weight, key_weight, value_weight, out_weight, key_cache, value_cache, lengths
):
    yz_count = lax.axis_size("yz")
    gx_count = lax.axis_size("gx")
    rows_here = lengths.shape[0]
    gathered = lax.all_gather(tokens, "yz", axis=0, tiled=True)
    all_rows = gathered.shape[0]
    flattened = gathered.reshape(all_rows * STEPS, gathered.shape[2])
    query_part = jnp.dot(flattened, query_weight, preferred_element_type=jnp.float32)
    key_part = jnp.dot(flattened, key_weight, preferred_element_type=jnp.float32)
    value_part = jnp.dot(flattened, value_weight, preferred_element_type=jnp.float32)
    arrived = (
        lax.all_to_all(
            query_part.reshape(yz_count * gx_count, rows_here, STEPS, 1, query_part.shape[1]),
            ("yz", "gx"),
            split_axis=0,
            concat_axis=3,
            tiled=True,
        ),
        lax.all_to_all(
            key_part.reshape(yz_count * gx_count, rows_here, STEPS, 1, key_part.shape[1]),
            ("yz", "gx"),
            split_axis=0,
            concat_axis=3,
            tiled=True,
        ),
        lax.all_to_all(
            value_part.reshape(yz_count * gx_count, rows_here, STEPS, 1, value_part.shape[1]),
            ("yz", "gx"),
            split_axis=0,
            concat_axis=3,
            tiled=True,
        ),
    )
    totals = [
        jnp.sum(member.reshape(rows_here, STEPS, yz_count, gx_count, member.shape[-1]), axis=3)
        for member in arrived
    ]
    queries = totals[0]
    key_sum = totals[1].reshape(rows_here, STEPS, HD)
    new_values = totals[2].reshape(rows_here, STEPS, HD).astype(jnp.bfloat16)
    positions = (lengths[:, None] + jnp.arange(STEPS, dtype=jnp.int32)[None, :]).astype(jnp.float32)
    rot_queries = rotate(queries, positions[:, :, None]).astype(jnp.bfloat16)
    new_keys = rotate(key_sum, positions).astype(jnp.bfloat16)
    scale_factor = HD ** (-0.5)
    cache_scores = (
        jnp.einsum("rshd,rkd->rshk", rot_queries, key_cache, preferred_element_type=jnp.float32)
        * scale_factor
    )
    new_scores = (
        jnp.einsum("rshd,rtd->rsht", rot_queries, new_keys, preferred_element_type=jnp.float32)
        * scale_factor
    )
    cache_probs, new_probs = normalize(cache_scores, new_scores, lengths, STEPS)
    head_out = jnp.einsum(
        "rshk,rkd->rshd", cache_probs, value_cache, preferred_element_type=jnp.float32
    )
    head_out = head_out + jnp.einsum(
        "rsht,rtd->rshd", new_probs, new_values, preferred_element_type=jnp.float32
    )
    head_out = head_out.astype(jnp.bfloat16)
    returned = lax.all_to_all(head_out, "yz", split_axis=2, concat_axis=0, tiled=True)
    paired = lax.all_gather(
        returned.reshape(yz_count, 1, rows_here, STEPS, HD), "gx", axis=1, tiled=True
    )
    head_rows = paired.reshape(all_rows, STEPS, HD)
    row_count = tokens.shape[0] * lax.axis_size("yz")
    product = jnp.dot(
        head_rows.reshape(row_count * STEPS, HD), out_weight, preferred_element_type=jnp.float32
    )
    return lax.psum_scatter(
        product.reshape(row_count, STEPS, out_weight.shape[1]).astype(jnp.bfloat16),
        "yz",
        scatter_dimension=0,
        tiled=True,
    )


FOLD = 4
CHUNKS = 3
AHEAD = 5
NZ = 4
NY = 2
MESH = pl.DeviceIdType.MESH


def place():
    me = lax.axis_index("yz")
    return me // NY, me % NY


def greet(z, y):
    barrier = pltpu.get_barrier_semaphore()
    pl.semaphore_signal(barrier, inc=1, device_id={"yz": z * NY + 1 - y}, device_id_type=MESH)

    @pl.when(z > 0)
    def _():
        pl.semaphore_signal(barrier, inc=1, device_id={"yz": (z - 1) * NY + y}, device_id_type=MESH)

    @pl.when(z < NZ - 1)
    def _():
        pl.semaphore_signal(barrier, inc=1, device_id={"yz": (z + 1) * NY + y}, device_id_type=MESH)

    pl.semaphore_wait(barrier, jnp.where(jnp.logical_and(z > 0, z < NZ - 1), 3, 2))


def gather_project_kernel(
    tokens_ref, qw_ref, kw_ref, vw_ref, q_out, kv_out,
    gathered, qw, kvw, w_sem, own_sem, up_send, down_send, side_send, recv,
):
    z, y = place()
    width = gathered.shape[3]
    rows = gathered.shape[2]
    features = qw.shape[0] // FOLD
    loads = [
        pltpu.make_async_copy(source, target, w_sem.at[i])
        for i, (source, target) in enumerate(
            (
                (qw_ref, qw),
                (kw_ref, kvw.at[pl.ds(0, kw_ref.shape[0]), :]),
                (vw_ref, kvw.at[pl.ds(kw_ref.shape[0], vw_ref.shape[0]), :]),
            )
        )
    ]
    own = [
        pltpu.make_async_copy(
            tokens_ref.at[:, pl.ds(c * width, width)], gathered.at[c, z * NY + y], own_sem.at[c]
        )
        for c in range(CHUNKS)
    ]
    for copy in own:
        copy.start()
    greet(z, y)

    def block(c, origin_z, origin_y, target, sem):
        origin = origin_z * NY + origin_y
        return pltpu.make_async_remote_copy(
            src_ref=gathered.at[c, origin],
            dst_ref=gathered.at[c, origin],
            send_sem=sem.at[c, origin_z],
            recv_sem=recv.at[c, origin],
            device_id={"yz": target},
            device_id_type=MESH,
        )

    side = z * NY + 1 - y

    def up(c, origin_z):
        return block(c, origin_z, y, (z + 1) * NY + y, up_send)

    def down(c, origin_z):
        return block(c, origin_z, y, (z - 1) * NY + y, down_send)

    def across(c, origin_z):
        return block(c, origin_z, y, side, side_send)

    def arrival(c, origin_z, origin_y):
        block(c, origin_z, origin_y, side, side_send).wait_recv()

    for c in range(CHUNKS):
        own[c].wait()

        @pl.when(z < NZ - 1)
        def _(c=c):
            up(c, z).start()

        @pl.when(z > 0)
        def _(c=c):
            down(c, z).start()

        across(c, z).start()
    for copy in loads:
        copy.start()

    def forward(c, k):
        @pl.when(z >= k)
        def _():
            arrival(c, z - k, y)

            @pl.when(z < NZ - 1)
            def _():
                up(c, z - k).start()

            across(c, z - k).start()

        @pl.when(z + k < NZ)
        def _():
            arrival(c, z + k, y)

            @pl.when(z > 0)
            def _():
                down(c, z + k).start()

            across(c, z + k).start()

    def multiply(c):
        for origin_z in range(NZ):
            arrival(c, origin_z, 1 - y)
        block_rows = gathered[c].reshape(NZ * NY * rows, width)
        fold = (lax.broadcasted_iota(jnp.int32, (NZ * NY * rows, 1), 0) % rows) // (rows // FOLD)
        def project(out, weigh):
            total = None
            for f in range(FOLD):
                term = weigh(pl.ds(f * features + c * width, width))
                total = term if f == 0 else jnp.where(fold == f, term, total)
            if c == 0:
                out[...] = total
            else:
                out[...] += total

        project(
            q_out,
            lambda at: jnp.dot(block_rows, qw[at, :], preferred_element_type=jnp.float32),
        )
        project(
            kv_out,
            lambda at: lax.dot_general(
                block_rows, kvw[:, at], (((1,), (1,)), ((), ())), preferred_element_type=jnp.float32
            ),
        )

    for slot in range(1, CHUNKS + NZ - 1):
        for c in range(CHUNKS):
            if 1 <= slot - c < NZ:
                forward(c, slot - c)
        done = slot - NZ
        if done == 0:
            for copy in loads:
                copy.wait()
        if done >= 0:
            multiply(done)
    multiply(CHUNKS - 1)

    for c in range(CHUNKS):
        for origin_z in range(NZ):
            across(c, origin_z).wait_send()

            @pl.when(jnp.logical_and(z < NZ - 1, origin_z <= z))
            def _(c=c, origin_z=origin_z):
                up(c, origin_z).wait_send()

            @pl.when(jnp.logical_and(z > 0, origin_z >= z))
            def _(c=c, origin_z=origin_z):
                down(c, origin_z).wait_send()


def gather_project(folded, query_weight, key_weight, value_weight):
    rows, features = folded.shape
    width = features // CHUNKS
    count = NZ * NY
    outs = [query_weight.shape[1], key_weight.shape[1] + value_weight.shape[1]]
    hbm = pl.BlockSpec(memory_space=pl.ANY)
    vmem = pl.BlockSpec(memory_space=pltpu.VMEM)
    dma = pltpu.SemaphoreType.DMA
    return pl.pallas_call(
        gather_project_kernel,
        out_shape=[jax.ShapeDtypeStruct((count * rows, n), jnp.float32) for n in outs],
        in_specs=[hbm] * 4,
        out_specs=[vmem] * 2,
        scratch_shapes=[
            pltpu.VMEM((CHUNKS, count, rows, width), jnp.bfloat16),
            pltpu.VMEM(query_weight.shape, jnp.bfloat16),
            pltpu.VMEM((outs[1], query_weight.shape[0]), jnp.bfloat16),
            dma((3,)),
            dma((CHUNKS,)),
            dma((CHUNKS, NZ)),
            dma((CHUNKS, NZ)),
            dma((CHUNKS, NZ)),
            dma((CHUNKS, count)),
        ],
        compiler_params=pltpu.CompilerParams(
            collective_id=0, has_side_effects=True, vmem_limit_bytes=48 * 1024 * 1024
        ),
        name="gather_project",
    )(folded, query_weight, key_weight.T, value_weight.T)


def project_scatter_kernel(
    heads_ref, weight_ref, out_ref,
    weight, terms, side_in, up_in, down_in,
    w_sem, side_send, side_recv, line_send, up_recv, down_recv,
):
    z, y = place()
    rows, width = terms.shape[2], terms.shape[3]
    depth = weight_ref.shape[0]
    features = weight_ref.shape[1] // FOLD
    loads = [
        [
            pltpu.make_async_copy(
                weight_ref.at[:, pl.ds(f * features + c * width, width)],
                weight.at[c, pl.ds(f * depth, depth), :],
                w_sem.at[c, f],
            )
            for f in range(FOLD)
        ]
        for c in range(CHUNKS)
    ]
    for group in loads:
        for copy in group:
            copy.start()
    greet(z, y)

    def across(c, dest):
        return pltpu.make_async_remote_copy(
            src_ref=terms.at[c, dest * NY + 1 - y],
            dst_ref=side_in.at[c, dest],
            send_sem=side_send.at[c, dest],
            recv_sem=side_recv.at[c, dest],
            device_id={"yz": z * NY + 1 - y},
            device_id_type=MESH,
        )

    def along(c, dest, step):
        return pltpu.make_async_remote_copy(
            src_ref=terms.at[c, dest * NY + y],
            dst_ref=(up_in if step > 0 else down_in).at[c, dest],
            send_sem=line_send.at[c, dest],
            recv_sem=(up_recv if step > 0 else down_recv).at[c, dest],
            device_id={"yz": (z + step) * NY + y},
            device_id_type=MESH,
        )

    def multiply(c):
        for copy in loads[c]:
            copy.wait()
        product = jnp.dot(heads_ref[...], weight[c], preferred_element_type=jnp.float32)
        terms[c] = product.astype(jnp.bfloat16).reshape(NZ * NY, rows, width)

    order = sorted(
        ((c, k) for c in range(CHUNKS) for k in range(NZ)), key=lambda g: (g[0] - g[1], g[0])
    )

    def each_side(group, act):
        c, k = order[group]
        if k == 0:
            act(across(c, z))
            return

        @pl.when(z + k < NZ)
        def _():
            act(across(c, z + k))

        @pl.when(z >= k)
        def _():
            act(across(c, z - k))

    def start_side(group):
        if group < CHUNKS * NZ:
            if order[group][1] == NZ - 1:
                multiply(order[group][0])
            each_side(group, lambda copy: copy.start())

    for group in range(AHEAD):
        start_side(group)

    def own_pair(c, dest):
        across(c, dest).wait_recv()
        return terms[c, dest * NY + y].astype(jnp.float32) + side_in[c, dest].astype(jnp.float32)

    def pass_on(c, dest, step, has_source):
        arrived = up_in if step > 0 else down_in
        total = own_pair(c, dest)
        terms[c, dest * NY + y] = total.astype(jnp.bfloat16)

        @pl.when(has_source)
        def _():
            along(c, dest, step).wait_recv()
            terms[c, dest * NY + y] = (total + arrived[c, dest].astype(jnp.float32)).astype(
                jnp.bfloat16
            )

        along(c, dest, step).start()

    for group, (c, k) in enumerate(order):
        each_side(group, lambda copy: copy.wait_send())
        start_side(group + AHEAD)
        if k > 0:
            @pl.when(z + k < NZ)
            def _(c=c, k=k):
                pass_on(c, z + k, 1, z > 0)

            @pl.when(z >= k)
            def _(c=c, k=k):
                pass_on(c, z - k, -1, z < NZ - 1)

            continue

        here = pl.ds(c * width, width)
        total = own_pair(c, z)

        @pl.when(z == 0)
        def _(c=c, here=here, total=total):
            along(c, z, -1).wait_recv()
            out_ref[:, here] = (total + down_in[c, z].astype(jnp.float32)).astype(jnp.bfloat16)

        @pl.when(z == NZ - 1)
        def _(c=c, here=here, total=total):
            along(c, z, 1).wait_recv()
            out_ref[:, here] = (total + up_in[c, z].astype(jnp.float32)).astype(jnp.bfloat16)

        @pl.when(jnp.logical_and(z > 0, z < NZ - 1))
        def _(c=c, here=here, total=total):
            along(c, z, 1).wait_recv()
            along(c, z, -1).wait_recv()
            out_ref[:, here] = (
                total + up_in[c, z].astype(jnp.float32) + down_in[c, z].astype(jnp.float32)
            ).astype(jnp.bfloat16)

    for c in range(CHUNKS):
        for dest in range(NZ):
            @pl.when(dest != z)
            def _(c=c, dest=dest):
                along(c, dest, 1).wait_send()


def project_scatter(heads, out_weight):
    depth, columns = out_weight.shape
    count = NZ * NY
    rows = heads.shape[0] // count
    width = columns // FOLD // CHUNKS
    dma = pltpu.SemaphoreType.DMA
    vmem = pl.BlockSpec(memory_space=pltpu.VMEM)
    landing = pltpu.VMEM((CHUNKS, NZ, rows, width), jnp.bfloat16)
    sems = dma((CHUNKS, NZ))
    return pl.pallas_call(
        project_scatter_kernel,
        out_shape=jax.ShapeDtypeStruct((rows, columns // FOLD), jnp.bfloat16),
        in_specs=[vmem, pl.BlockSpec(memory_space=pl.ANY)],
        out_specs=vmem,
        scratch_shapes=[
            pltpu.VMEM((CHUNKS, FOLD * depth, width), jnp.bfloat16),
            pltpu.VMEM((CHUNKS, count, rows, width), jnp.bfloat16),
            landing,
            landing,
            landing,
            dma((CHUNKS, FOLD)),
            sems,
            sems,
            sems,
            sems,
            sems,
        ],
        compiler_params=pltpu.CompilerParams(
            collective_id=1, has_side_effects=True, vmem_limit_bytes=48 * 1024 * 1024
        ),
        name="project_scatter",
    )(heads, out_weight)


def attend(queries, key_sum, new_values, key_cache, value_cache, lengths):
    positions = (lengths[:, None] + jnp.arange(STEPS, dtype=jnp.int32)[None, :]).astype(jnp.float32)
    rot_queries = rotate(queries, positions[:, :, None]).astype(jnp.bfloat16)
    new_keys = rotate(key_sum, positions).astype(jnp.bfloat16)
    scale_factor = HD ** (-0.5)
    cache_scores = (
        jnp.einsum("rshd,rkd->rshk", rot_queries, key_cache, preferred_element_type=jnp.float32)
        * scale_factor
    )
    new_scores = (
        jnp.einsum("rshd,rtd->rsht", rot_queries, new_keys, preferred_element_type=jnp.float32)
        * scale_factor
    )
    cache_probs, new_probs = normalize(cache_scores, new_scores, lengths, STEPS)
    head_out = jnp.einsum(
        "rshk,rkd->rshd", cache_probs, value_cache, preferred_element_type=jnp.float32
    )
    head_out = head_out + jnp.einsum(
        "rsht,rtd->rshd", new_probs, new_values, preferred_element_type=jnp.float32
    )
    return head_out.astype(jnp.bfloat16)


def local_line(
    tokens, query_weight, key_weight, value_weight, out_weight, key_cache, value_cache, lengths
):
    yz_count = lax.axis_size("yz")
    gx_count = lax.axis_size("gx")
    rows_here = lengths.shape[0]
    owned = tokens.shape[0] * STEPS
    features = tokens.shape[2]
    folded = (
        tokens.reshape(owned, FOLD, features // FOLD)
        .transpose(1, 0, 2)
        .reshape(FOLD * owned, features // FOLD)
    )
    parts = gather_project(folded, query_weight, key_weight, value_weight)
    joined = jnp.concatenate(parts, axis=1)
    joined = joined.reshape(yz_count, FOLD, owned, joined.shape[1]).sum(axis=1)
    arrived = lax.all_to_all(
        joined.reshape(yz_count * gx_count, rows_here * STEPS, joined.shape[-1]),
        ("yz", "gx"),
        split_axis=0,
        concat_axis=0,
        tiled=True,
    )
    totals = arrived.reshape(yz_count, gx_count, rows_here, STEPS, -1).sum(axis=1)
    totals = totals.transpose(1, 2, 0, 3)
    key_columns = key_weight.shape[1]
    queries = totals[..., :HD]
    key_sum = totals[..., HD : HD + key_columns].reshape(rows_here, STEPS, HD)
    new_values = totals[..., HD + key_columns :].reshape(rows_here, STEPS, HD).astype(jnp.bfloat16)
    head_out = attend(queries, key_sum, new_values, key_cache, value_cache, lengths)
    by_head = head_out.reshape(rows_here * STEPS, yz_count, HD).transpose(1, 0, 2)
    sent = jnp.broadcast_to(by_head[:, None], (yz_count, gx_count) + by_head.shape[1:])
    returned = lax.all_to_all(
        sent.reshape(yz_count * gx_count, rows_here * STEPS, HD),
        ("yz", "gx"),
        split_axis=0,
        concat_axis=0,
        tiled=True,
    )
    heads = returned.reshape(yz_count, 1, owned, 1, HD)
    same = jnp.eye(FOLD, dtype=bool)[None, :, None, :, None]
    heads = jnp.where(same, heads, jnp.bfloat16(0)).reshape(yz_count * FOLD * owned, FOLD * HD)
    summed = project_scatter(heads, out_weight)
    return (
        summed.reshape(FOLD, owned, -1).transpose(1, 0, 2).reshape(tokens.shape[0], STEPS, features)
    )


def solution(mesh):
    body = local_line if mesh.shape["yz"] == NZ * NY and mesh.shape["gx"] == 2 else local
    placed = (
        P(("rep", "yz"), None, "gx"),
        P("gx", "yz"),
        P("gx", "yz"),
        P("gx", "yz"),
        P("yz", "gx"),
        P(("rep", "yz", "gx"), None, None),
        P(("rep", "yz", "gx"), None, None),
        P(("rep", "yz", "gx")),
    )
    return jax.shard_map(
        body, mesh=mesh, in_specs=placed, out_specs=P(("rep", "yz"), None, "gx"), check_vma=False
    )
```

```python
import math

import jax
import jax.numpy as jnp
from jax import lax
from jax.experimental import pallas as pl
from jax.experimental.pallas import tpu as pltpu
from jax.sharding import PartitionSpec as P

HD = 256
STEPS = 3


def rotate(values, positions):
    half_dim = values.shape[-1] // 2
    frequency = jnp.exp(jnp.arange(half_dim, dtype=jnp.float32) * (-math.log(10000.0) / half_dim))
    angles = positions[..., None] * frequency
    cosine = jnp.cos(angles)
    sine_part = jnp.sin(angles)
    front_half = values[..., :half_dim]
    back_half = values[..., half_dim:]
    return jnp.concatenate(
        [front_half * cosine - back_half * sine_part, back_half * cosine + front_half * sine_part],
        axis=-1,
    )


def normalize(cache_scores, new_scores, lengths, steps_count):
    cache_len = cache_scores.shape[-1]
    cache_live = (jnp.arange(cache_len, dtype=jnp.int32)[None, :] < lengths[:, None])[
        :, None, None, :
    ]
    new_live = (
        jnp.arange(steps_count, dtype=jnp.int32)[None, :]
        <= jnp.arange(steps_count, dtype=jnp.int32)[:, None]
    )[None, :, None, :]
    floor_value = jnp.float32(-1e30)
    cache_scores = jnp.where(cache_live, cache_scores, floor_value)
    new_scores = jnp.where(new_live, new_scores, floor_value)
    highest = jnp.maximum(
        jnp.max(cache_scores, axis=-1, keepdims=True), jnp.max(new_scores, axis=-1, keepdims=True)
    )
    cache_exp = jnp.exp(cache_scores - highest)
    new_exp = jnp.exp(new_scores - highest)
    denominator = jnp.sum(cache_exp, axis=-1, keepdims=True) + jnp.sum(
        new_exp, axis=-1, keepdims=True
    )
    return (
        (cache_exp / denominator).astype(jnp.bfloat16),
        (new_exp / denominator).astype(jnp.bfloat16),
    )


def local(
    tokens, query_weight, key_weight, value_weight, out_weight, key_cache, value_cache, lengths
):
    yz_count = lax.axis_size("yz")
    gx_count = lax.axis_size("gx")
    rows_here = lengths.shape[0]
    gathered = lax.all_gather(tokens, "yz", axis=0, tiled=True)
    all_rows = gathered.shape[0]
    flattened = gathered.reshape(all_rows * STEPS, gathered.shape[2])
    query_part = jnp.dot(flattened, query_weight, preferred_element_type=jnp.float32)
    key_part = jnp.dot(flattened, key_weight, preferred_element_type=jnp.float32)
    value_part = jnp.dot(flattened, value_weight, preferred_element_type=jnp.float32)
    arrived = (
        lax.all_to_all(
            query_part.reshape(yz_count * gx_count, rows_here, STEPS, 1, query_part.shape[1]),
            ("yz", "gx"),
            split_axis=0,
            concat_axis=3,
            tiled=True,
        ),
        lax.all_to_all(
            key_part.reshape(yz_count * gx_count, rows_here, STEPS, 1, key_part.shape[1]),
            ("yz", "gx"),
            split_axis=0,
            concat_axis=3,
            tiled=True,
        ),
        lax.all_to_all(
            value_part.reshape(yz_count * gx_count, rows_here, STEPS, 1, value_part.shape[1]),
            ("yz", "gx"),
            split_axis=0,
            concat_axis=3,
            tiled=True,
        ),
    )
    totals = [
        jnp.sum(member.reshape(rows_here, STEPS, yz_count, gx_count, member.shape[-1]), axis=3)
        for member in arrived
    ]
    queries = totals[0]
    key_sum = totals[1].reshape(rows_here, STEPS, HD)
    new_values = totals[2].reshape(rows_here, STEPS, HD).astype(jnp.bfloat16)
    positions = (lengths[:, None] + jnp.arange(STEPS, dtype=jnp.int32)[None, :]).astype(jnp.float32)
    rot_queries = rotate(queries, positions[:, :, None]).astype(jnp.bfloat16)
    new_keys = rotate(key_sum, positions).astype(jnp.bfloat16)
    scale_factor = HD ** (-0.5)
    cache_scores = (
        jnp.einsum("rshd,rkd->rshk", rot_queries, key_cache, preferred_element_type=jnp.float32)
        * scale_factor
    )
    new_scores = (
        jnp.einsum("rshd,rtd->rsht", rot_queries, new_keys, preferred_element_type=jnp.float32)
        * scale_factor
    )
    cache_probs, new_probs = normalize(cache_scores, new_scores, lengths, STEPS)
    head_out = jnp.einsum(
        "rshk,rkd->rshd", cache_probs, value_cache, preferred_element_type=jnp.float32
    )
    head_out = head_out + jnp.einsum(
        "rsht,rtd->rshd", new_probs, new_values, preferred_element_type=jnp.float32
    )
    head_out = head_out.astype(jnp.bfloat16)
    returned = lax.all_to_all(head_out, "yz", split_axis=2, concat_axis=0, tiled=True)
    paired = lax.all_gather(
        returned.reshape(yz_count, 1, rows_here, STEPS, HD), "gx", axis=1, tiled=True
    )
    head_rows = paired.reshape(all_rows, STEPS, HD)
    row_count = tokens.shape[0] * lax.axis_size("yz")
    product = jnp.dot(
        head_rows.reshape(row_count * STEPS, HD), out_weight, preferred_element_type=jnp.float32
    )
    return lax.psum_scatter(
        product.reshape(row_count, STEPS, out_weight.shape[1]).astype(jnp.bfloat16),
        "yz",
        scatter_dimension=0,
        tiled=True,
    )


FOLD = 4
CHUNKS = 6
AHEAD = 8
NZ = 4
NY = 2
MESH = pl.DeviceIdType.MESH


def place():
    me = lax.axis_index("yz")
    return me // NY, me % NY


def greet(z, y):
    barrier = pltpu.get_barrier_semaphore()
    pl.semaphore_signal(barrier, inc=1, device_id={"yz": z * NY + 1 - y}, device_id_type=MESH)

    @pl.when(z > 0)
    def _():
        pl.semaphore_signal(barrier, inc=1, device_id={"yz": (z - 1) * NY + y}, device_id_type=MESH)

    @pl.when(z < NZ - 1)
    def _():
        pl.semaphore_signal(barrier, inc=1, device_id={"yz": (z + 1) * NY + y}, device_id_type=MESH)

    pl.semaphore_wait(barrier, jnp.where(jnp.logical_and(z > 0, z < NZ - 1), 3, 2))


def gather_project_kernel(
    tokens_ref, qw_ref, kw_ref, vw_ref, q_out, kv_out,
    gathered, qw, kvw, w_sem, own_sem, up_send, down_send, side_send, recv,
):
    z, y = place()
    width = gathered.shape[3]
    rows = gathered.shape[2]
    features = qw.shape[0] // FOLD
    loads = [
        pltpu.make_async_copy(source, target, w_sem.at[i])
        for i, (source, target) in enumerate(
            (
                (qw_ref, qw),
                (kw_ref, kvw.at[pl.ds(0, kw_ref.shape[0]), :]),
                (vw_ref, kvw.at[pl.ds(kw_ref.shape[0], vw_ref.shape[0]), :]),
            )
        )
    ]
    own = [
        pltpu.make_async_copy(
            tokens_ref.at[:, pl.ds(c * width, width)], gathered.at[c, z * NY + y], own_sem.at[c]
        )
        for c in range(CHUNKS)
    ]
    for copy in own:
        copy.start()
    greet(z, y)

    def block(c, origin_z, origin_y, target, sem):
        origin = origin_z * NY + origin_y
        return pltpu.make_async_remote_copy(
            src_ref=gathered.at[c, origin],
            dst_ref=gathered.at[c, origin],
            send_sem=sem.at[c, origin_z],
            recv_sem=recv.at[c, origin],
            device_id={"yz": target},
            device_id_type=MESH,
        )

    side = z * NY + 1 - y

    def up(c, origin_z):
        return block(c, origin_z, y, (z + 1) * NY + y, up_send)

    def down(c, origin_z):
        return block(c, origin_z, y, (z - 1) * NY + y, down_send)

    def across(c, origin_z):
        return block(c, origin_z, y, side, side_send)

    def arrival(c, origin_z, origin_y):
        block(c, origin_z, origin_y, side, side_send).wait_recv()

    for c in range(CHUNKS):
        own[c].wait()

        @pl.when(z < NZ - 1)
        def _(c=c):
            up(c, z).start()

        @pl.when(z > 0)
        def _(c=c):
            down(c, z).start()

        across(c, z).start()
    for copy in loads:
        copy.start()

    def forward(c, k):
        @pl.when(z >= k)
        def _():
            arrival(c, z - k, y)

            @pl.when(z < NZ - 1)
            def _():
                up(c, z - k).start()

            across(c, z - k).start()

        @pl.when(z + k < NZ)
        def _():
            arrival(c, z + k, y)

            @pl.when(z > 0)
            def _():
                down(c, z + k).start()

            across(c, z + k).start()

    def multiply(c):
        for origin_z in range(NZ):
            arrival(c, origin_z, 1 - y)
        block_rows = gathered[c].reshape(NZ * NY * rows, width)
        fold = (lax.broadcasted_iota(jnp.int32, (NZ * NY * rows, 1), 0) % rows) // (rows // FOLD)
        def project(out, weigh):
            total = None
            for f in range(FOLD):
                term = weigh(pl.ds(f * features + c * width, width))
                total = term if f == 0 else jnp.where(fold == f, term, total)
            if c == 0:
                out[...] = total
            else:
                out[...] += total

        project(
            q_out,
            lambda at: jnp.dot(block_rows, qw[at, :], preferred_element_type=jnp.float32),
        )
        project(
            kv_out,
            lambda at: lax.dot_general(
                block_rows, kvw[:, at], (((1,), (1,)), ((), ())), preferred_element_type=jnp.float32
            ),
        )

    for slot in range(1, CHUNKS + NZ - 1):
        for c in range(CHUNKS):
            if 1 <= slot - c < NZ:
                forward(c, slot - c)
        done = slot - NZ
        if done == 0:
            for copy in loads:
                copy.wait()
        if done >= 0:
            multiply(done)
    multiply(CHUNKS - 1)

    for c in range(CHUNKS):
        for origin_z in range(NZ):
            across(c, origin_z).wait_send()

            @pl.when(jnp.logical_and(z < NZ - 1, origin_z <= z))
            def _(c=c, origin_z=origin_z):
                up(c, origin_z).wait_send()

            @pl.when(jnp.logical_and(z > 0, origin_z >= z))
            def _(c=c, origin_z=origin_z):
                down(c, origin_z).wait_send()


def gather_project(folded, query_weight, key_weight, value_weight):
    rows, features = folded.shape
    width = features // CHUNKS
    count = NZ * NY
    outs = [query_weight.shape[1], key_weight.shape[1] + value_weight.shape[1]]
    hbm = pl.BlockSpec(memory_space=pl.ANY)
    vmem = pl.BlockSpec(memory_space=pltpu.VMEM)
    dma = pltpu.SemaphoreType.DMA
    return pl.pallas_call(
        gather_project_kernel,
        out_shape=[jax.ShapeDtypeStruct((count * rows, n), jnp.float32) for n in outs],
        in_specs=[hbm] * 4,
        out_specs=[vmem] * 2,
        scratch_shapes=[
            pltpu.VMEM((CHUNKS, count, rows, width), jnp.bfloat16),
            pltpu.VMEM(query_weight.shape, jnp.bfloat16),
            pltpu.VMEM((outs[1], query_weight.shape[0]), jnp.bfloat16),
            dma((3,)),
            dma((CHUNKS,)),
            dma((CHUNKS, NZ)),
            dma((CHUNKS, NZ)),
            dma((CHUNKS, NZ)),
            dma((CHUNKS, count)),
        ],
        compiler_params=pltpu.CompilerParams(
            collective_id=0, has_side_effects=True, vmem_limit_bytes=60 * 1024 * 1024
        ),
        name="gather_project",
    )(folded, query_weight, key_weight.T, value_weight.T)


def project_scatter_kernel(
    heads_ref, weight_ref, out_ref,
    weight, terms, side_in, up_in, down_in,
    w_sem, side_send, side_recv, line_send, up_recv, down_recv,
):
    z, y = place()
    rows, width = terms.shape[2], terms.shape[3]
    depth = weight_ref.shape[0]
    features = weight_ref.shape[1] // FOLD
    loads = [
        [
            pltpu.make_async_copy(
                weight_ref.at[:, pl.ds(f * features + c * width, width)],
                weight.at[c, pl.ds(f * depth, depth), :],
                w_sem.at[c, f],
            )
            for f in range(FOLD)
        ]
        for c in range(CHUNKS)
    ]
    for group in loads:
        for copy in group:
            copy.start()
    greet(z, y)

    def across(c, dest):
        return pltpu.make_async_remote_copy(
            src_ref=terms.at[c, dest * NY + 1 - y],
            dst_ref=side_in.at[c, dest],
            send_sem=side_send.at[c, dest],
            recv_sem=side_recv.at[c, dest],
            device_id={"yz": z * NY + 1 - y},
            device_id_type=MESH,
        )

    def along(c, dest, step):
        return pltpu.make_async_remote_copy(
            src_ref=terms.at[c, dest * NY + y],
            dst_ref=(up_in if step > 0 else down_in).at[c, dest],
            send_sem=line_send.at[c, dest],
            recv_sem=(up_recv if step > 0 else down_recv).at[c, dest],
            device_id={"yz": (z + step) * NY + y},
            device_id_type=MESH,
        )

    def multiply(c):
        for copy in loads[c]:
            copy.wait()
        product = jnp.dot(heads_ref[...], weight[c], preferred_element_type=jnp.float32)
        terms[c] = product.astype(jnp.bfloat16).reshape(NZ * NY, rows, width)

    order = sorted(
        ((c, k) for c in range(CHUNKS) for k in range(NZ)), key=lambda g: (g[0] - g[1], g[0])
    )

    def each_side(group, act):
        c, k = order[group]
        if k == 0:
            act(across(c, z))
            return

        @pl.when(z + k < NZ)
        def _():
            act(across(c, z + k))

        @pl.when(z >= k)
        def _():
            act(across(c, z - k))

    def start_side(group):
        if group < CHUNKS * NZ:
            if order[group][1] == NZ - 1:
                multiply(order[group][0])
            each_side(group, lambda copy: copy.start())

    for group in range(AHEAD):
        start_side(group)

    def own_pair(c, dest):
        across(c, dest).wait_recv()
        return terms[c, dest * NY + y].astype(jnp.float32) + side_in[c, dest].astype(jnp.float32)

    def pass_on(c, dest, step, has_source):
        arrived = up_in if step > 0 else down_in
        total = own_pair(c, dest)
        terms[c, dest * NY + y] = total.astype(jnp.bfloat16)

        @pl.when(has_source)
        def _():
            along(c, dest, step).wait_recv()
            terms[c, dest * NY + y] = (total + arrived[c, dest].astype(jnp.float32)).astype(
                jnp.bfloat16
            )

        along(c, dest, step).start()

    for group, (c, k) in enumerate(order):
        each_side(group, lambda copy: copy.wait_send())
        start_side(group + AHEAD)
        if k > 0:
            @pl.when(z + k < NZ)
            def _(c=c, k=k):
                pass_on(c, z + k, 1, z > 0)

            @pl.when(z >= k)
            def _(c=c, k=k):
                pass_on(c, z - k, -1, z < NZ - 1)

            continue

        here = pl.ds(c * width, width)
        total = own_pair(c, z)

        @pl.when(z == 0)
        def _(c=c, here=here, total=total):
            along(c, z, -1).wait_recv()
            out_ref[:, here] = (total + down_in[c, z].astype(jnp.float32)).astype(jnp.bfloat16)

        @pl.when(z == NZ - 1)
        def _(c=c, here=here, total=total):
            along(c, z, 1).wait_recv()
            out_ref[:, here] = (total + up_in[c, z].astype(jnp.float32)).astype(jnp.bfloat16)

        @pl.when(jnp.logical_and(z > 0, z < NZ - 1))
        def _(c=c, here=here, total=total):
            along(c, z, 1).wait_recv()
            along(c, z, -1).wait_recv()
            out_ref[:, here] = (
                total + up_in[c, z].astype(jnp.float32) + down_in[c, z].astype(jnp.float32)
            ).astype(jnp.bfloat16)

    for c in range(CHUNKS):
        for dest in range(NZ):
            @pl.when(dest != z)
            def _(c=c, dest=dest):
                along(c, dest, 1).wait_send()


def project_scatter(heads, out_weight):
    depth, columns = out_weight.shape
    count = NZ * NY
    rows = heads.shape[0] // count
    width = columns // FOLD // CHUNKS
    dma = pltpu.SemaphoreType.DMA
    vmem = pl.BlockSpec(memory_space=pltpu.VMEM)
    landing = pltpu.VMEM((CHUNKS, NZ, rows, width), jnp.bfloat16)
    sems = dma((CHUNKS, NZ))
    return pl.pallas_call(
        project_scatter_kernel,
        out_shape=jax.ShapeDtypeStruct((rows, columns // FOLD), jnp.bfloat16),
        in_specs=[vmem, pl.BlockSpec(memory_space=pl.ANY)],
        out_specs=vmem,
        scratch_shapes=[
            pltpu.VMEM((CHUNKS, FOLD * depth, width), jnp.bfloat16),
            pltpu.VMEM((CHUNKS, count, rows, width), jnp.bfloat16),
            landing,
            landing,
            landing,
            dma((CHUNKS, FOLD)),
            sems,
            sems,
            sems,
            sems,
            sems,
        ],
        compiler_params=pltpu.CompilerParams(
            collective_id=1, has_side_effects=True, vmem_limit_bytes=60 * 1024 * 1024
        ),
        name="project_scatter",
    )(heads, out_weight)


def attend(queries, key_sum, new_values, key_cache, value_cache, lengths):
    positions = (lengths[:, None] + jnp.arange(STEPS, dtype=jnp.int32)[None, :]).astype(jnp.float32)
    rot_queries = rotate(queries, positions[:, :, None]).astype(jnp.bfloat16)
    new_keys = rotate(key_sum, positions).astype(jnp.bfloat16)
    scale_factor = HD ** (-0.5)
    cache_scores = (
        jnp.einsum("rshd,rkd->rshk", rot_queries, key_cache, preferred_element_type=jnp.float32)
        * scale_factor
    )
    new_scores = (
        jnp.einsum("rshd,rtd->rsht", rot_queries, new_keys, preferred_element_type=jnp.float32)
        * scale_factor
    )
    cache_probs, new_probs = normalize(cache_scores, new_scores, lengths, STEPS)
    head_out = jnp.einsum(
        "rshk,rkd->rshd", cache_probs, value_cache, preferred_element_type=jnp.float32
    )
    head_out = head_out + jnp.einsum(
        "rsht,rtd->rshd", new_probs, new_values, preferred_element_type=jnp.float32
    )
    return head_out.astype(jnp.bfloat16)


def local_line(
    tokens, query_weight, key_weight, value_weight, out_weight, key_cache, value_cache, lengths
):
    yz_count = lax.axis_size("yz")
    gx_count = lax.axis_size("gx")
    rows_here = lengths.shape[0]
    owned = tokens.shape[0] * STEPS
    features = tokens.shape[2]
    folded = (
        tokens.reshape(owned, FOLD, features // FOLD)
        .transpose(1, 0, 2)
        .reshape(FOLD * owned, features // FOLD)
    )
    parts = gather_project(folded, query_weight, key_weight, value_weight)
    joined = jnp.concatenate(parts, axis=1)
    joined = joined.reshape(yz_count, FOLD, owned, joined.shape[1]).sum(axis=1)
    arrived = lax.all_to_all(
        joined.reshape(yz_count * gx_count, rows_here * STEPS, joined.shape[-1]),
        ("yz", "gx"),
        split_axis=0,
        concat_axis=0,
        tiled=True,
    )
    totals = arrived.reshape(yz_count, gx_count, rows_here, STEPS, -1).sum(axis=1)
    totals = totals.transpose(1, 2, 0, 3)
    key_columns = key_weight.shape[1]
    queries = totals[..., :HD]
    key_sum = totals[..., HD : HD + key_columns].reshape(rows_here, STEPS, HD)
    new_values = totals[..., HD + key_columns :].reshape(rows_here, STEPS, HD).astype(jnp.bfloat16)
    head_out = attend(queries, key_sum, new_values, key_cache, value_cache, lengths)
    by_head = head_out.reshape(rows_here * STEPS, yz_count, HD).transpose(1, 0, 2)
    sent = jnp.broadcast_to(by_head[:, None], (yz_count, gx_count) + by_head.shape[1:])
    returned = lax.all_to_all(
        sent.reshape(yz_count * gx_count, rows_here * STEPS, HD),
        ("yz", "gx"),
        split_axis=0,
        concat_axis=0,
        tiled=True,
    )
    heads = returned.reshape(yz_count, 1, owned, 1, HD)
    same = jnp.eye(FOLD, dtype=bool)[None, :, None, :, None]
    heads = jnp.where(same, heads, jnp.bfloat16(0)).reshape(yz_count * FOLD * owned, FOLD * HD)
    summed = project_scatter(heads, out_weight)
    return (
        summed.reshape(FOLD, owned, -1).transpose(1, 0, 2).reshape(tokens.shape[0], STEPS, features)
    )


def solution(mesh):
    body = local_line if mesh.shape["yz"] == NZ * NY and mesh.shape["gx"] == 2 else local
    placed = (
        P(("rep", "yz"), None, "gx"),
        P("gx", "yz"),
        P("gx", "yz"),
        P("gx", "yz"),
        P("yz", "gx"),
        P(("rep", "yz", "gx"), None, None),
        P(("rep", "yz", "gx"), None, None),
        P(("rep", "yz", "gx")),
    )
    return jax.shard_map(
        body, mesh=mesh, in_specs=placed, out_specs=P(("rep", "yz"), None, "gx"), check_vma=False
    )
```
